128 devices in a mesh: blk: 16 (over y_lo, z, core), row: 8 (over y_hi, x).
Axes of the slice: x: 4, y: 4 (y_hi: 2, y_lo: 2; y = y_hi * 2 + y_lo), z: 4, core: 2. Of those that a mesh axis runs over, the one named last changes fastest.
Arguments:
- image_embed: float32 [32768, 768], P(('blk', 'row')), may hold values from -16 to 16, as said below
- text_embed: float32 [32768, 768], P(('blk', 'row')), may hold values from -4 to 4
- logit_scale: float32 [1], replicated, may hold values from 7 to 14
Outputs:
- loss: float32 [1], replicated
- scale_grad: float32 [1], replicated
- image_grad: float32 [32768, 768], P(('blk', 'row'))
- text_grad: float32 [32768, 768], P(('blk', 'row'))
The draws below stay inside these ranges and needn't reach their ends.
Inputs may be any that keep to these rules, and one draw needn't show every extreme that they name: Row i of image_embed and row i of text_embed describe the same pair.
All inputs are finite; a program needn't handle non-finite values.
Results may differ from the reference program's by a relative error of at most 0.0003.
Values sent between devices are 32-bit elements; how exact they have to be, the bound alone decides.
A program may use at most 128 MiB of HBM per device.

```python
import math
import jax
import jax.numpy as jnp
from jax import lax

EMBED = 768
WINDOW = 4
GROUP = 2048
PAIRS = 32768
N_BLK = 16


def make_pairs(key, strength):
    keys = jax.random.split(key, 9)
    root = math.sqrt(EMBED)
    image_dir = jax.random.normal(keys[0], (PAIRS, EMBED), jnp.float32) / root
    noise = jax.random.normal(keys[1], (PAIRS, EMBED), jnp.float32) / root
    text_dir = 0.6 * image_dir + 0.8 * noise
    ramp = 0.5 + jnp.arange(PAIRS, dtype=jnp.float32)[:, None] / PAIRS
    image_size = jnp.exp(jax.random.uniform(keys[2], (PAIRS, 1), jnp.float32, math.log(0.3), math.log(3.0))) * ramp
    text_size = jnp.exp(jax.random.uniform(keys[3], (PAIRS, 1), jnp.float32, math.log(0.3), math.log(3.0))) * ramp
    images = image_size * image_dir
    texts = text_size * text_dir
    half_count = PAIRS // 2
    chosen = jax.random.uniform(keys[5], (half_count, 1), jnp.float32) < strength / 64.0
    factor = jax.random.uniform(keys[6], (half_count, 1), jnp.float32, 15.0, 60.0)
    base_rows = text_dir[0::2]
    base_rows = base_rows / jnp.sqrt(jnp.sum(base_rows * base_rows, axis=1, keepdims=True))
    nudge = 0.2 / factor
    extra_text = jax.random.normal(keys[7], (half_count, EMBED), jnp.float32) * (0.5 / root)
    extra_text = extra_text - jnp.sum(extra_text * base_rows, axis=1, keepdims=True) * base_rows
    extra_image = jax.random.normal(keys[8], (half_count, EMBED), jnp.float32) * (0.3 / root)
    extra_image = extra_image - jnp.sum(extra_image * base_rows, axis=1, keepdims=True) * base_rows
    odd_text = (1.0 + nudge) * base_rows + extra_text
    even_image = factor * base_rows
    odd_image = factor * ((1.0 + nudge) * base_rows + extra_image)
    aligned_text = jnp.stack([base_rows, odd_text], axis=1).reshape(PAIRS, EMBED)
    aligned_image = jnp.stack([even_image, odd_image], axis=1).reshape(PAIRS, EMBED)
    row_mask = jnp.repeat(chosen, 2, axis=0)
    images = jnp.where(row_mask, aligned_image, images)
    texts = jnp.where(row_mask, aligned_text, texts)
    return (jnp.clip(images, -16.0, 16.0), jnp.clip(texts, -4.0, 4.0))


def draw_image_embed(key, part):
    strength = 0.0
    return make_pairs(key, strength)[0]


def draw_text_embed(key, part):
    strength = 0.0
    return make_pairs(key, strength)[1]


def setup_inputs(seed: int = 0) -> dict:
    key_list = jax.random.split(jax.random.key(seed), 4)
    image_embed = draw_image_embed(jax.random.fold_in(key_list[3], 71), 0)
    text_embed = draw_text_embed(jax.random.fold_in(key_list[3], 71), 0)
    logit_scale = jnp.clip(jnp.exp(jax.random.uniform(key_list[2], (1,), jnp.float32, math.log(7.0), math.log(14.0))), 7.0, 14.0)
    return {"image_embed": image_embed, "text_embed": text_embed, "logit_scale": logit_scale}


def reference(image_embed, text_embed, logit_scale):
    scale_value = logit_scale[0]
    image_groups = image_embed.reshape(N_BLK, GROUP, EMBED)
    text_groups = text_embed.reshape(N_BLK, GROUP, EMBED)
    offsets = jnp.arange(WINDOW, dtype=jnp.int32)

    def window_texts(group_index):
        picked = (group_index + offsets) % N_BLK
        return jnp.take(text_groups, picked, axis=0).reshape(WINDOW * GROUP, EMBED)

    def group_images(group_index):
        return jnp.take(image_groups, group_index, axis=0)

    def raw_products(group_index):
        return lax.dot_general(group_images(group_index), window_texts(group_index),
                               (((1,), (1,)), ((), ())), precision=lax.Precision.HIGHEST,
                               preferred_element_type=jnp.float32)

    def first_pass(group_index):
        scores = scale_value * raw_products(group_index)
        row_top = jnp.max(scores, axis=1)
        row_lse = row_top + jnp.log(jnp.sum(jnp.exp(scores - row_top[:, None]), axis=1))
        col_top = jnp.max(scores, axis=0)
        col_total = jnp.sum(jnp.exp(scores - col_top[None, :]), axis=0)
        return row_lse, col_top.reshape(WINDOW, GROUP), col_total.reshape(WINDOW, GROUP)

    all_groups = jnp.arange(N_BLK, dtype=jnp.int32)
    image_lse, col_top, col_total = lax.map(first_pass, all_groups)
    source = (all_groups[:, None] - offsets[None, :]) % N_BLK
    parts_top = col_top[source, offsets[None, :]]
    parts_total = col_total[source, offsets[None, :]]
    overall_top = jnp.max(parts_top, axis=1)
    text_lse = overall_top + jnp.log(jnp.sum(parts_total * jnp.exp(parts_top - overall_top[:, None, :]), axis=1))

    def second_pass(state_pair, group_index):
        text_sum, scale_sum = state_pair
        raw_dot = raw_products(group_index)
        scores = scale_value * raw_dot
        lse_rows = jnp.take(image_lse, group_index, axis=0)
        lse_cols = jnp.take(text_lse, (group_index + offsets) % N_BLK, axis=0).reshape(WINDOW * GROUP)
        weight = 0.5 * jnp.exp(scores - lse_rows[:, None]) + 0.5 * jnp.exp(scores - lse_cols[None, :])
        image_part = scale_value * jnp.dot(weight, window_texts(group_index), precision=lax.Precision.HIGHEST,
                                           preferred_element_type=jnp.float32)
        text_part = scale_value * lax.dot_general(weight, group_images(group_index), (((0,), (0,)), ((), ())),
                                                  precision=lax.Precision.HIGHEST,
                                                  preferred_element_type=jnp.float32)
        text_sum = text_sum.at[(group_index + offsets) % N_BLK].add(text_part.reshape(WINDOW, GROUP, EMBED))
        scale_sum = scale_sum + jnp.sum(weight * raw_dot)
        return (text_sum, scale_sum), image_part

    start_state = (jnp.zeros((N_BLK, GROUP, EMBED), jnp.float32), jnp.zeros((), jnp.float32))
    (text_sum, scale_sum), image_sum = lax.scan(second_pass, start_state, all_groups)
    positive = jnp.sum(image_embed * text_embed, axis=1)
    image_grad = image_sum.reshape(PAIRS, EMBED) - scale_value * text_embed
    text_grad = text_sum.reshape(PAIRS, EMBED) - scale_value * image_embed
    loss = (0.5 * jnp.sum(image_lse) + 0.5 * jnp.sum(text_lse) - scale_value * jnp.sum(positive)) / PAIRS
    scale_grad = (scale_sum - jnp.sum(positive)) / PAIRS
    return loss.reshape(1), scale_grad.reshape(1), image_grad, text_grad
```

```python
import functools

import jax
import jax.numpy as jnp
from jax import lax
from jax.experimental import pallas as pl
from jax.experimental.pallas import tpu as pltpu
from jax.sharding import PartitionSpec as P

MESH = pl.DeviceIdType.MESH
F32 = jnp.float32
BF16 = jnp.bfloat16
WINDOW = 4
N_IMG = 4
OFFSETS = (0, 1, 3, 2)
N_TXT = 8
LOW = -1e30

DELTAS = [(d, g) for d in (-3, -2, -1, 0, 1, 2, 3) for g in (0, 1) if (d, g) != (0, 0)]


class Place:
    def __init__(self, y_lo, z, core, y_hi, x):
        self.y_lo, self.z, self.core, self.y_hi, self.x = y_lo, z, core, y_hi, x

    def device(self):
        return (self.y_lo * 8 + self.z * 2 + self.core, self.y_hi * 4 + self.x)

    def move(self, x=0, h=0, c=0, z=0, yl=0, blk=0, plane=0):
        y_lo, zz, core = self.y_lo, self.z, self.core
        if blk:
            b = lax.rem(y_lo * 8 + zz * 2 + core + blk + 16, 16)
            y_lo, zz, core = b // 8, lax.rem(b // 2, 4), lax.rem(b, 2)
        if plane:
            k = lax.rem(y_lo * 4 + zz + plane + 8, 8)
            y_lo, zz = k // 4, lax.rem(k, 4)
        if z:
            zz = lax.rem(zz + z + 4, 4)
        if c:
            core = 1 - core
        if yl:
            y_lo = 1 - y_lo
        y_hi = 1 - self.y_hi if h else self.y_hi
        xx = lax.rem(self.x + x + 4, 4) if x else self.x
        return Place(y_lo, zz, core, y_hi, xx)


def here():
    b, r = lax.axis_index("blk"), lax.axis_index("row")
    return Place(b // 8, lax.rem(b // 2, 4), lax.rem(b, 2), r // 4, lax.rem(r, 4))


def split(value):
    high = value.astype(BF16)
    return high, (value - high.astype(F32)).astype(BF16)


def kernel(
    rows,
    scale_ref,
    img_ref,
    txt_ref,
    sums_ref,
    img_out,
    txt_out,
    img_in,
    txt_in,
    relay_in,
    img_hi,
    img_lo,
    txt_hi,
    txt_lo,
    scores,
    r_hi,
    r_lo,
    row_top,
    row_sum,
    row_stat,
    col_stat,
    row_got,
    col_got,
    img_part,
    txt_part,
    chip_got,
    ring_got,
    relay_got,
    relay_back,
    pair_got,
    img_got,
    img_half,
    sum_send,
    sum_got,
    send_sem,
    recv_sem,
):
    me = here()
    is0, is1 = me.core == 0, me.core == 1
    half = rows // 2
    top, bottom = pl.ds(0, half), pl.ds(half, half)
    scale = scale_ref[0]
    pending = []
    slots = {}

    def sem(name):
        return slots.setdefault(name, len(slots))

    def copy(name, src, dst, place):
        return pltpu.make_async_remote_copy(
            src_ref=src,
            dst_ref=dst,
            send_sem=send_sem.at[len(pending)],
            recv_sem=recv_sem.at[sem(name)],
            device_id=place.device(),
            device_id_type=MESH,
        )

    def send(name, src, dst, place, when=None):
        c = copy(name, src, dst, place)
        if when is None:
            c.start()
        else:
            pl.when(when)(c.start)
        pending.append((c, when))

    def arrive(name, dst, when=None):
        c = copy(name, dst, dst, me.move(h=1))
        if when is None:
            c.wait_recv()
        else:
            pl.when(when)(c.wait_recv)

    source_plane_from_relay = me.move(z=-1)
    relay_to = source_plane_from_relay.move(plane=-2)
    relay_to = Place(relay_to.y_lo, relay_to.z, 1 - me.core, me.y_hi, me.x)
    relay_from = me.move(plane=2).move(z=1)
    relay_from = Place(relay_from.y_lo, relay_from.z, 1 - me.core, me.y_hi, me.x)

    partners = [me.move(x=1), me.move(x=2), me.move(x=3), me.move(h=1), me.move(c=1)]
    partners += [me.move(z=1), me.move(z=2), me.move(z=3), me.move(yl=1)]
    partners += [relay_to, relay_to.move(h=1), relay_from, relay_from.move(h=1)]
    partners += [me.move(blk=d, h=g) for d, g in DELTAS if d != 0]
    barrier = pltpu.get_barrier_semaphore()
    for p in partners:
        pl.semaphore_signal(barrier, inc=1, device_id=p.device(), device_id_type=MESH)
    pl.semaphore_wait(barrier, len(partners))

    def tx(d, e):
        return txt_in.at[2 * d + e - 1]

    at0 = me.z == 0
    not0 = me.z != 0
    prev = [me.move(blk=-1), me.move(blk=-2)]
    send("i1", img_ref, img_in.at[0], me.move(x=-1))
    send("i2", img_ref, img_in.at[1], me.move(x=1))
    send("t01", txt_ref, tx(0, 1), me.move(h=1))
    send("t10", txt_ref, tx(1, 0), me.move(blk=-1))
    send("t20", txt_ref, tx(2, 0), me.move(blk=-2), is1)
    send("relay", txt_ref, relay_in, me.move(z=1), is0)
    send("t11", txt_ref, tx(1, 1), me.move(blk=-1, h=1), is0 & at0)
    send("t21", txt_ref, tx(2, 1), me.move(blk=-2, h=1), is1 & at0)

    def img_ready(i, value):
        high, low = split(value)
        at = pl.ds(i * rows, rows)
        img_hi[at, :] = high
        img_lo[at, :] = low

    def txt_ready(t, value):
        high, low = split(value)
        at = pl.ds(t * rows, rows)
        txt_hi[at, :] = high
        txt_lo[at, :] = low

    row_top[...] = jnp.full(row_top.shape, LOW, F32)
    row_sum[...] = jnp.zeros(row_sum.shape, F32)
    img_ready(0, img_ref[...])
    txt_ready(0, txt_ref[...])

    nt = (((1,), (1,)), ((), ()))
    tn = (((0,), (0,)), ((), ()))
    nn = (((1,), (0,)), ((), ()))

    def dot(a, b, dims):
        return lax.dot_general(a, b, dims, preferred_element_type=F32)

    def score_tiles(t, first, last):
        cols = pl.ds(t * rows, rows)

        def tile(i, carry):
            at = pl.ds(pl.multiple_of(i * rows, rows), rows)
            raw = dot(img_hi[at, :], txt_hi[cols, :], nt)
            raw += dot(img_hi[at, :], txt_lo[cols, :], nt)
            raw += dot(img_lo[at, :], txt_hi[cols, :], nt)
            scores[at, cols] = scale * raw
            return carry

        lax.fori_loop(first, last, tile, 0)

    def block_stats(t):
        cols = pl.ds(t * rows, rows)

        def tops(i, carry):
            at = pl.ds(pl.multiple_of(i * rows, rows), rows)
            s = scores[at, cols]
            s0, s1 = s[:, :128], s[:, 128:]
            old = row_top[at, :]
            new = jnp.maximum(old, jnp.maximum(s0, s1))
            row_sum[at, :] = (
                row_sum[at, :] * jnp.exp(old - new) + jnp.exp(s0 - new) + jnp.exp(s1 - new)
            )
            row_top[at, :] = new
            return jnp.maximum(carry, jnp.max(s, axis=0, keepdims=True))

        ctop = lax.fori_loop(0, N_IMG, tops, jnp.full((1, rows), LOW, F32))

        def totals(i, carry):
            at = pl.ds(pl.multiple_of(i * rows, rows), rows)
            return carry + jnp.sum(jnp.exp(scores[at, cols] - ctop), axis=0, keepdims=True)

        csum = lax.fori_loop(0, N_IMG, totals, jnp.zeros((1, rows), F32))
        col_stat[t : t + 1, :] = ctop
        col_stat[N_TXT + t : N_TXT + t + 1, :] = csum

    def text_block(d, e):
        arrive(f"t{d}{e}", tx(d, e))
        txt_ready(2 * d + e, tx(d, e)[...])

    score_tiles(0, 0, 1)
    arrive("relay", relay_in, is0)
    send("t30", relay_in, tx(3, 0), relay_to, is0)
    send("t31", relay_in, tx(3, 1), relay_to.move(h=1), is0)
    arrive("i1", img_in.at[0])
    send("i3a", img_in.at[0, top], img_in.at[2, top], me.move(x=-1))
    arrive("i2", img_in.at[1])
    send("i3b", img_in.at[1, bottom], img_in.at[2, bottom], me.move(x=1))
    text_block(0, 1)
    send("t11", tx(0, 1), tx(1, 1), me.move(blk=-1), is1 | not0)
    send("t21", tx(0, 1), tx(2, 1), me.move(blk=-2), is1 & not0)
    text_block(1, 0)
    send("t20", tx(1, 0), tx(2, 0), me.move(c=1), is1)
    img_ready(1, img_in[0])
    img_ready(2, img_in[1])
    score_tiles(0, 1, 3)
    text_block(2, 0)
    send("t30", tx(2, 0), tx(3, 0), me.move(c=1), is1)
    score_tiles(1, 0, 3)
    score_tiles(2, 0, 3)
    score_tiles(4, 0, 3)
    arrive("i3a", img_in.at[2, top])
    arrive("i3b", img_in.at[2, bottom])
    img_ready(3, img_in[2])
    for t in (0, 1, 2, 4):
        score_tiles(t, 3, 4)
        block_stats(t)
    text_block(3, 0)
    score_tiles(6, 0, 4)
    block_stats(6)
    text_block(1, 1)
    send("t21", tx(1, 1), tx(2, 1), me.move(c=1), is1)
    score_tiles(3, 0, 4)
    block_stats(3)
    text_block(2, 1)
    send("t31", tx(2, 1), tx(3, 1), me.move(c=1), is1)
    score_tiles(5, 0, 4)
    block_stats(5)
    text_block(3, 1)
    score_tiles(7, 0, 4)
    block_stats(7)

    for n, (d, g) in enumerate(DELTAS):
        m = DELTAS.index((-d, g))
        send(f"c{m}", col_stat, col_got.at[m], me.move(blk=d, h=g))
    for i in range(N_IMG):
        at = pl.ds(i * rows, rows)
        m = jnp.transpose(row_top[at, :])
        s = jnp.transpose(row_sum[at, :])
        best = jnp.max(m, axis=0, keepdims=True)
        row_stat[i : i + 1, :] = best
        row_stat[N_IMG + i : N_IMG + i + 1, :] = jnp.sum(s * jnp.exp(m - best), axis=0, keepdims=True)
    for o in (1, 2, 3):
        send(f"r{4 - o}", row_stat, row_got.at[4 - o - 1], me.move(x=o))
    for n in range(len(DELTAS)):
        arrive(f"c{n}", col_got.at[n])
    for o in (1, 2, 3):
        arrive(f"r{o}", row_got.at[o - 1])

    def join(parts):
        best = functools.reduce(jnp.maximum, [m for m, _ in parts])
        return best + jnp.log(sum(s * jnp.exp(m - best) for m, s in parts))

    text_lse = []
    for t in range(N_TXT):
        d, e = t // 2, t % 2
        parts = [(col_stat[t : t + 1, :], col_stat[N_TXT + t : N_TXT + t + 1, :])]
        for n, (dd, g) in enumerate(DELTAS):
            if 0 <= d - dd < WINDOW:
                u = 2 * (d - dd) + (1 - e if g else e)
                parts.append((col_got[n, u : u + 1, :], col_got[n, N_TXT + u : N_TXT + u + 1, :]))
        text_lse.append(join(parts))
    loss_part = 0.5 * text_lse[0]
    for i in range(N_IMG):
        parts = [(row_stat[i : i + 1, :], row_stat[N_IMG + i : N_IMG + i + 1, :])]
        for o in (1, 2, 3):
            u = OFFSETS.index((OFFSETS[i] - o) % 4)
            parts.append((row_got[o - 1, u : u + 1, :], row_got[o - 1, N_IMG + u : N_IMG + u + 1, :]))
        lse = join(parts)
        if i == 0:
            loss_part += 0.5 * lse
        row_top[pl.ds(i * rows, rows), :] = jnp.transpose(jnp.broadcast_to(lse, (128, rows)))

    diagonal = lax.broadcasted_iota(jnp.int32, (rows, rows), 0) == lax.broadcasted_iota(
        jnp.int32, (rows, rows), 1
    )
    own = scores[pl.ds(0, rows), pl.ds(0, rows)]
    loss_part -= jnp.sum(jnp.where(diagonal, own, 0.0), axis=0, keepdims=True)
    scale_part = jnp.zeros((1, rows), F32)

    def weigh(t, scale_part):
        cols = pl.ds(t * rows, rows)

        def tile(i, carry):
            at = pl.ds(pl.multiple_of(i * rows, rows), rows)
            s = scores[at, cols]
            lse = row_top[at, :]
            by_row = jnp.exp(s - jnp.concatenate([lse, lse], axis=1))
            w = 0.5 * (by_row + jnp.exp(s - text_lse[t]))
            if t == 0:
                w = jnp.where(diagonal & (i == 0), w - 1.0, w)
            r_hi[at, cols], r_lo[at, cols] = split(w)
            return carry + jnp.sum(w * s, axis=0, keepdims=True)

        return lax.fori_loop(0, N_IMG, tile, scale_part)

    def text_partial(d, e):
        t = 2 * d + e
        cols = pl.ds(t * rows, rows)

        def part(n, carry):
            wide = pl.ds(pl.multiple_of(n * 256, 256), 256)
            acc = dot(r_hi[:, cols], img_hi[:, wide], tn)
            acc += dot(r_hi[:, cols], img_lo[:, wide], tn)
            acc += dot(r_lo[:, cols], img_hi[:, wide], tn)
            txt_part[t, :, wide] = acc
            return carry

        lax.fori_loop(0, img_ref.shape[1] // 256, part, 0)

    def image_partial(i):
        at = pl.ds(i * rows, rows)

        def part(n, carry):
            wide = pl.ds(pl.multiple_of(n * 256, 256), 256)
            acc = dot(r_hi[at, :], txt_hi[:, wide], nn)
            acc += dot(r_hi[at, :], txt_lo[:, wide], nn)
            acc += dot(r_lo[at, :], txt_hi[:, wide], nn)
            img_part[i, :, wide] = acc
            return carry

        lax.fori_loop(0, img_ref.shape[1] // 256, part, 0)

    def add(dst, src):
        dst[...] += src[...]

    def gp(d, e):
        return txt_part.at[2 * d + e]

    for t in (7, 6, 5, 4, 3, 2, 1, 0):
        scale_part = weigh(t, scale_part)

    at3 = me.z == 3

    def up(d, e, distance):
        if e == 0:
            send(f"a{e}", gp(d, e), ring_got.at[e], me.move(blk=distance), is1)
        else:
            send(f"a{e}", gp(d, e), ring_got.at[e], me.move(blk=distance), is1 & (me.z != 3))
            send(f"a{e}", gp(d, e), ring_got.at[e], me.move(blk=distance, h=1), is1 & at3)

    def chip(d, e):
        send(f"g{d}{e}", gp(d + 1, e), chip_got.at[2 * d + e], me.move(c=1), is0)

    def chip_add(d, e):
        @pl.when(is1)
        def _():
            copy(f"g{d}{e}", gp(d, e), chip_got.at[2 * d + e], me.move(c=1)).wait_recv()
            add(gp(d, e), chip_got.at[2 * d + e])

    for e in (1, 0):
        text_partial(3, e)
        chip(2, e)
        send(f"b{e}", gp(3, e), relay_got.at[e], relay_from.move(h=e), is1)
    for e in (1, 0):
        text_partial(2, e)
        chip(1, e)
        chip_add(2, e)
        up(2, e, 2)
    image_partial(3)
    send("p3a", img_part.at[3, top], img_half.at[0], me.move(x=1))
    send("p3b", img_part.at[3, bottom], img_half.at[1], me.move(x=-1))
    for e in (1, 0):
        text_partial(1, e)
        chip(0, e)
        chip_add(1, e)
        up(1, e, 1)
    image_partial(1)
    send("p1b", img_part.at[1, bottom], img_got.at[0, bottom], me.move(x=1))
    image_partial(2)
    send("p2a", img_part.at[2, top], img_got.at[1, top], me.move(x=-1))

    @pl.when(is0)
    def _():
        copy("b0", relay_got.at[0], relay_got.at[0], me.move(h=1)).wait_recv()
        copy("b1", relay_got.at[1], relay_got.at[1], me.move(h=1)).wait_recv()
        add(relay_got.at[0], relay_got.at[1])

    send("back", relay_got.at[0], relay_back, me.move(z=-1), is0)
    text_partial(0, 1)
    arrive("p3a", img_half.at[0])
    add(img_part.at[1, top], img_half.at[0])
    send("p1a", img_part.at[1, top], img_got.at[0, top], me.move(x=1))
    arrive("p3b", img_half.at[1])
    add(img_part.at[2, bottom], img_half.at[1])
    send("p2b", img_part.at[2, bottom], img_got.at[1, bottom], me.move(x=-1))
    chip_add(0, 1)
    arrive("a1", ring_got.at[1])

    @pl.when(not0)
    def _():
        add(gp(0, 1), ring_got.at[1])

    send("y", gp(0, 1), pair_got, me.move(h=1))
    text_partial(0, 0)
    chip_add(0, 0)

    @pl.when(at0)
    def _():
        add(gp(0, 0), ring_got.at[1])

    image_partial(0)

    loss_sum = jnp.sum(loss_part, axis=1, keepdims=True)
    scale_sum = jnp.sum(scale_part, axis=1, keepdims=True) / scale
    line = lax.broadcasted_iota(jnp.int32, (8, 128), 0)
    total = jnp.where(line == 0, loss_sum, scale_sum)
    stages = [
        [me.move(c=1)],
        [me.move(h=1)],
        [me.move(yl=1)],
        [me.move(x=1), me.move(x=2), me.move(x=3)],
        [me.move(z=1), me.move(z=2), me.move(z=3)],
    ]
    n = 0
    for level, peers in enumerate(stages):
        sum_send[level] = total
        for j, p in enumerate(peers):
            send(f"s{n + j}", sum_send.at[level], sum_got.at[n + j], p)
        for j in range(len(peers)):
            arrive(f"s{n + j}", sum_got.at[n + j])
            total = total + sum_got[n + j]
        n += len(peers)
    pairs = rows * lax.axis_size("blk") * lax.axis_size("row")
    sums_ref[...] = total / pairs

    arrive("a0", ring_got.at[0])
    arrive("back", relay_back, is0)

    @pl.when(is0)
    def _():
        add(gp(0, 0), relay_back)

    for name, at, j in (("p1b", bottom, 0), ("p2a", top, 1), ("p1a", top, 0), ("p2b", bottom, 1)):
        arrive(name, img_got.at[j, at])
    img_out[...] = scale * (img_part[0] + img_got[0] + img_got[1])
    arrive("y", pair_got)
    txt_out[...] = scale * (txt_part[0] + ring_got[0] + pair_got[...])

    for c, when in pending:
        if when is None:
            c.wait_send()
        else:
            pl.when(when)(c.wait_send)


N_SEM = 80


def shards(image_embed, text_embed, logit_scale):
    rows, width = image_embed.shape
    block = (rows, width)
    vmem = pl.BlockSpec(memory_space=pltpu.VMEM)
    sums, image_grad, text_grad = pl.pallas_call(
        functools.partial(kernel, rows),
        out_shape=(
            jax.ShapeDtypeStruct((8, 128), F32),
            jax.ShapeDtypeStruct(block, F32),
            jax.ShapeDtypeStruct(block, F32),
        ),
        in_specs=[pl.BlockSpec(memory_space=pltpu.SMEM), vmem, vmem],
        out_specs=(vmem, vmem, vmem),
        scratch_shapes=[
            pltpu.VMEM((3, *block), F32),
            pltpu.VMEM((7, *block), F32),
            pltpu.VMEM(block, F32),
            pltpu.VMEM((N_IMG * rows, width), BF16),
            pltpu.VMEM((N_IMG * rows, width), BF16),
            pltpu.VMEM((N_TXT * rows, width), BF16),
            pltpu.VMEM((N_TXT * rows, width), BF16),
            pltpu.VMEM((N_IMG * rows, N_TXT * rows), F32),
            pltpu.VMEM((N_IMG * rows, N_TXT * rows), BF16),
            pltpu.VMEM((N_IMG * rows, N_TXT * rows), BF16),
            pltpu.VMEM((N_IMG * rows, 128), F32),
            pltpu.VMEM((N_IMG * rows, 128), F32),
            pltpu.VMEM((2 * N_IMG, rows), F32),
            pltpu.VMEM((2 * N_TXT, rows), F32),
            pltpu.VMEM((3, 2 * N_IMG, rows), F32),
            pltpu.VMEM((len(DELTAS), 2 * N_TXT, rows), F32),
            pltpu.VMEM((N_IMG, *block), F32),
            pltpu.VMEM((N_TXT, *block), F32),
            pltpu.VMEM((6, *block), F32),
            pltpu.VMEM((2, *block), F32),
            pltpu.VMEM((2, *block), F32),
            pltpu.VMEM(block, F32),
            pltpu.VMEM(block, F32),
            pltpu.VMEM((2, *block), F32),
            pltpu.VMEM((2, rows // 2, width), F32),
            pltpu.VMEM((5, 8, 128), F32),
            pltpu.VMEM((9, 8, 128), F32),
            pltpu.SemaphoreType.DMA((N_SEM,)),
            pltpu.SemaphoreType.DMA((N_SEM,)),
        ],
        compiler_params=pltpu.CompilerParams(
            collective_id=0, has_side_effects=True, vmem_limit_bytes=62 << 20
        ),
        cost_estimate=pl.CostEstimate(flops=29 * 10**9, bytes_accessed=4 * 10**6, transcendentals=10**7),
    )(logit_scale, image_embed, text_embed)
    return sums[0, :1], sums[1, :1], image_grad, text_grad


def solution(mesh):
    in_specs = (P(("blk", "row"), None), P(("blk", "row"), None), P())
    out_specs = (P(), P(), P(("blk", "row"), None), P(("blk", "row"), None))
    return jax.shard_map(shards, mesh=mesh, in_specs=in_specs, out_specs=out_specs, check_vma=False)
```

```python
import functools

import jax
import jax.numpy as jnp
from jax import lax
from jax.experimental import pallas as pl
from jax.experimental.pallas import tpu as pltpu
from jax.sharding import PartitionSpec as P

MESH = pl.DeviceIdType.MESH
F32 = jnp.float32
BF16 = jnp.bfloat16
WINDOW = 4
N_IMG = 4
OFFSETS = (0, 1, 3, 2)
N_TXT = 8
LOW = -1e30

DELTAS = [(d, g) for d in (-3, -2, -1, 0, 1, 2, 3) for g in (0, 1) if (d, g) != (0, 0)]


class Place:
    def __init__(self, y_lo, z, core, y_hi, x):
        self.y_lo, self.z, self.core, self.y_hi, self.x = y_lo, z, core, y_hi, x

    def device(self):
        return (self.y_lo * 8 + self.z * 2 + self.core, self.y_hi * 4 + self.x)

    def move(self, x=0, h=0, c=0, z=0, yl=0, blk=0, plane=0):
        y_lo, zz, core = self.y_lo, self.z, self.core
        if blk:
            b = lax.rem(y_lo * 8 + zz * 2 + core + blk + 16, 16)
            y_lo, zz, core = b // 8, lax.rem(b // 2, 4), lax.rem(b, 2)
        if plane:
            k = lax.rem(y_lo * 4 + zz + plane + 8, 8)
            y_lo, zz = k // 4, lax.rem(k, 4)
        if z:
            zz = lax.rem(zz + z + 4, 4)
        if c:
            core = 1 - core
        if yl:
            y_lo = 1 - y_lo
        y_hi = 1 - self.y_hi if h else self.y_hi
        xx = lax.rem(self.x + x + 4, 4) if x else self.x
        return Place(y_lo, zz, core, y_hi, xx)


def here():
    b, r = lax.axis_index("blk"), lax.axis_index("row")
    return Place(b // 8, lax.rem(b // 2, 4), lax.rem(b, 2), r // 4, lax.rem(r, 4))


def split(value):
    high = value.astype(BF16)
    return high, (value - high.astype(F32)).astype(BF16)


def kernel(
    rows,
    scale_ref,
    img_ref,
    txt_ref,
    sums_ref,
    img_out,
    txt_out,
    img_in,
    txt_in,
    relay_in,
    img_hi,
    img_lo,
    txt_hi,
    txt_lo,
    scores,
    r_hi,
    r_lo,
    row_top,
    row_sum,
    row_stat,
    col_stat,
    row_got,
    col_got,
    img_part,
    txt_part,
    chip_got,
    ring_got,
    relay_got,
    relay_back,
    pair_got,
    img_got,
    img_half,
    sum_send,
    sum_got,
    send_sem,
    recv_sem,
):
    me = here()
    is0, is1 = me.core == 0, me.core == 1
    half = rows // 2
    top, bottom = pl.ds(0, half), pl.ds(half, half)
    scale = scale_ref[0]
    pending = []
    slots = {}

    def sem(name):
        return slots.setdefault(name, len(slots))

    def copy(name, src, dst, place):
        return pltpu.make_async_remote_copy(
            src_ref=src,
            dst_ref=dst,
            send_sem=send_sem.at[len(pending)],
            recv_sem=recv_sem.at[sem(name)],
            device_id=place.device(),
            device_id_type=MESH,
        )

    def send(name, src, dst, place, when=None):
        c = copy(name, src, dst, place)
        if when is None:
            c.start()
        else:
            pl.when(when)(c.start)
        pending.append((c, when))

    def arrive(name, dst, when=None):
        c = copy(name, dst, dst, me.move(h=1))
        if when is None:
            c.wait_recv()
        else:
            pl.when(when)(c.wait_recv)

    def pieces(name, src, dst, place, when=None):
        send(name + "a", src.at[top], dst.at[top], place, when)
        send(name + "b", src.at[bottom], dst.at[bottom], place, when)

    def arrive_pieces(name, dst, when=None):
        arrive(name + "a", dst.at[top], when)
        arrive(name + "b", dst.at[bottom], when)

    relay_to = me.move(z=-1).move(plane=-2).move(c=1)
    relay_from = me.move(plane=2).move(z=1).move(c=1)
    back_to = me.move(z=1).move(plane=2).move(c=1)
    back_from = me.move(plane=-2).move(z=-1).move(c=1)
    crossing = (me.z == 1) | (me.z == 2)

    partners = [me.move(x=1), me.move(x=2), me.move(x=3), me.move(h=1), me.move(c=1)]
    partners += [me.move(z=1), me.move(z=2), me.move(z=3), me.move(yl=1)]
    partners += [relay_from, relay_from.move(h=1), back_from, back_from.move(h=1)]
    partners += [me.move(blk=d, h=g) for d, g in DELTAS if d != 0]
    barrier = pltpu.get_barrier_semaphore()
    for p in partners:
        pl.semaphore_signal(barrier, inc=1, device_id=p.device(), device_id_type=MESH)
    pl.semaphore_wait(barrier, len(partners))

    def tx(d, e):
        return txt_in.at[2 * d + e - 1]

    at0 = me.z == 0
    not0 = me.z != 0
    prev = [me.move(blk=-1), me.move(blk=-2)]
    at3 = me.z == 3
    pieces("t10", txt_ref, tx(1, 0), me.move(blk=-1), is1 | not0)
    early = len(pending)
    pieces("t10", txt_ref, tx(1, 0), me.move(blk=-1), is0 & at0)
    pieces("t20", txt_ref, tx(2, 0), me.move(blk=-2), is1 & at0)
    pieces("t20", txt_ref, tx(2, 0), me.move(blk=-2), is1 & not0)
    pieces("r0", txt_ref, relay_in.at[0], me.move(z=1), is0)
    pieces("t01", txt_ref, tx(0, 1), me.move(h=1), not0)
    pieces("i1", img_ref, img_in.at[0], me.move(x=-1))
    pieces("i2", img_ref, img_in.at[1], me.move(x=1))

    def img_ready(i, value):
        high, low = split(value)
        at = pl.ds(i * rows, rows)
        img_hi[at, :] = high
        img_lo[at, :] = low

    def txt_ready(t, value):
        high, low = split(value)
        at = pl.ds(t * rows, rows)
        txt_hi[at, :] = high
        txt_lo[at, :] = low

    row_top[...] = jnp.full(row_top.shape, LOW, F32)
    row_sum[...] = jnp.zeros(row_sum.shape, F32)
    img_ready(0, img_ref[...])
    txt_ready(0, txt_ref[...])

    nt = (((1,), (1,)), ((), ()))
    tn = (((0,), (0,)), ((), ()))
    nn = (((1,), (0,)), ((), ()))

    def dot(a, b, dims):
        return lax.dot_general(a, b, dims, preferred_element_type=F32)

    def score_tiles(t, first, last):
        cols = pl.ds(t * rows, rows)

        def tile(i, carry):
            at = pl.ds(pl.multiple_of(i * rows, rows), rows)
            raw = dot(img_hi[at, :], txt_hi[cols, :], nt)
            raw += dot(img_hi[at, :], txt_lo[cols, :], nt)
            raw += dot(img_lo[at, :], txt_hi[cols, :], nt)
            scores[at, cols] = scale * raw
            return carry

        lax.fori_loop(first, last, tile, 0, unroll=True)

    def block_stats(t):
        cols = pl.ds(t * rows, rows)

        def tops(i, carry):
            at = pl.ds(pl.multiple_of(i * rows, rows), rows)
            s = scores[at, cols]
            s0, s1 = s[:, :128], s[:, 128:]
            old = row_top[at, :]
            new = jnp.maximum(old, jnp.maximum(s0, s1))
            row_sum[at, :] = (
                row_sum[at, :] * jnp.exp(old - new) + jnp.exp(s0 - new) + jnp.exp(s1 - new)
            )
            row_top[at, :] = new
            return jnp.maximum(carry, jnp.max(s, axis=0, keepdims=True))

        ctop = lax.fori_loop(0, N_IMG, tops, jnp.full((1, rows), LOW, F32), unroll=True)

        def totals(i, carry):
            at = pl.ds(pl.multiple_of(i * rows, rows), rows)
            return carry + jnp.sum(jnp.exp(scores[at, cols] - ctop), axis=0, keepdims=True)

        csum = lax.fori_loop(0, N_IMG, totals, jnp.zeros((1, rows), F32), unroll=True)
        col_stat[t : t + 1, :] = ctop
        col_stat[N_TXT + t : N_TXT + t + 1, :] = csum

    def text_block(d, e):
        arrive_pieces(f"t{d}{e}", tx(d, e))
        txt_ready(2 * d + e, tx(d, e)[...])

    def scored(t):
        score_tiles(t, 0, N_IMG)
        block_stats(t)

    score_tiles(0, 0, 1)
    for p, at in (("a", top), ("b", bottom)):
        arrive("r0" + p, relay_in.at[0, at], is0)
        send("t30" + p, relay_in.at[0, at], tx(3, 0).at[at], relay_to, is0)
        send("t31" + p, relay_in.at[0, at], tx(3, 1).at[at], relay_to.move(h=1), is0 & crossing)
    for i in range(early, early + 4):
        c, when = pending[i]
        pl.when(when)(c.wait_send)
        pending[i] = None
    pieces("t01", txt_ref, tx(0, 1), me.move(h=1), at0)
    for p, at in (("a", top), ("b", bottom)):
        arrive("t01" + p, tx(0, 1).at[at])
        send("t11" + p, tx(0, 1).at[at], tx(1, 1).at[at], me.move(blk=-1), is1 | not0)
        send("t21" + p, tx(0, 1).at[at], tx(2, 1).at[at], me.move(blk=-2), is1 & not0)
        send("r1" + p, tx(0, 1).at[at], relay_in.at[1, at], me.move(z=1), is0 & (me.z >= 2))
    arrive("i1a", img_in.at[0, top])
    send("i3a", img_in.at[0, top], img_in.at[2, top], me.move(x=-1))
    arrive("i2b", img_in.at[1, bottom])
    send("i3b", img_in.at[1, bottom], img_in.at[2, bottom], me.move(x=1))
    txt_ready(1, tx(0, 1)[...])
    score_tiles(1, 0, 1)
    for d in (1, 2):
        for p, at in (("a", top), ("b", bottom)):
            arrive(f"t{d}0{p}", tx(d, 0).at[at])
            send(f"t{d + 1}0{p}", tx(d, 0).at[at], tx(d + 1, 0).at[at], me.move(c=1), is1)
            send(f"t{d}1{p}", tx(d, 0).at[at], tx(d, 1).at[at], me.move(h=1), is1 & at3)
        txt_ready(2 * d, tx(d, 0)[...])
    arrive("i1b", img_in.at[0, bottom])
    arrive("i2a", img_in.at[1, top])
    img_ready(1, img_in[0])
    img_ready(2, img_in[1])
    score_tiles(0, 1, 3)
    score_tiles(1, 1, 3)
    for p, at in (("a", top), ("b", bottom)):
        arrive("r1" + p, relay_in.at[1, at], is0 & ~crossing)
        send("t31" + p, relay_in.at[1, at], tx(3, 1).at[at], relay_to, is0 & ~crossing)
    arrive("i3a", img_in.at[2, top])
    arrive("i3b", img_in.at[2, bottom])
    img_ready(3, img_in[2])
    for t in (0, 1):
        score_tiles(t, 3, 4)
        block_stats(t)
    scored(2)
    scored(4)
    text_block(3, 0)
    scored(6)
    text_block(1, 1)
    pieces("t21", tx(1, 1), tx(2, 1), me.move(c=1), is1)
    text_block(2, 1)
    pieces("t31", tx(2, 1), tx(3, 1), me.move(c=1), is1)
    scored(3)
    scored(5)
    text_block(3, 1)
    scored(7)

    for n, (d, g) in enumerate(DELTAS):
        m = DELTAS.index((-d, g))
        send(f"c{m}", col_stat, col_got.at[m], me.move(blk=d, h=g))
    for i in range(N_IMG):
        at = pl.ds(i * rows, rows)
        m = jnp.transpose(row_top[at, :])
        s = jnp.transpose(row_sum[at, :])
        best = jnp.max(m, axis=0, keepdims=True)
        row_stat[i : i + 1, :] = best
        row_stat[N_IMG + i : N_IMG + i + 1, :] = jnp.sum(s * jnp.exp(m - best), axis=0, keepdims=True)
    for o in (1, 2, 3):
        send(f"r{4 - o}", row_stat, row_got.at[4 - o - 1], me.move(x=o))
    for n in range(len(DELTAS)):
        arrive(f"c{n}", col_got.at[n])
    for o in (1, 2, 3):
        arrive(f"r{o}", row_got.at[o - 1])

    def join(parts):
        best = functools.reduce(jnp.maximum, [m for m, _ in parts])
        return best + jnp.log(sum(s * jnp.exp(m - best) for m, s in parts))

    text_lse = []
    for t in range(N_TXT):
        d, e = t // 2, t % 2
        parts = [(col_stat[t : t + 1, :], col_stat[N_TXT + t : N_TXT + t + 1, :])]
        for n, (dd, g) in enumerate(DELTAS):
            if 0 <= d - dd < WINDOW:
                u = 2 * (d - dd) + (1 - e if g else e)
                parts.append((col_got[n, u : u + 1, :], col_got[n, N_TXT + u : N_TXT + u + 1, :]))
        text_lse.append(join(parts))
    loss_part = 0.5 * text_lse[0]
    for i in range(N_IMG):
        parts = [(row_stat[i : i + 1, :], row_stat[N_IMG + i : N_IMG + i + 1, :])]
        for o in (1, 2, 3):
            u = OFFSETS.index((OFFSETS[i] - o) % 4)
            parts.append((row_got[o - 1, u : u + 1, :], row_got[o - 1, N_IMG + u : N_IMG + u + 1, :]))
        lse = join(parts)
        if i == 0:
            loss_part += 0.5 * lse
        row_top[pl.ds(i * rows, rows), :] = jnp.transpose(jnp.broadcast_to(lse, (128, rows)))

    diagonal = lax.broadcasted_iota(jnp.int32, (rows, rows), 0) == lax.broadcasted_iota(
        jnp.int32, (rows, rows), 1
    )
    own = scores[pl.ds(0, rows), pl.ds(0, rows)]
    loss_part -= jnp.sum(jnp.where(diagonal, own, 0.0), axis=0, keepdims=True)
    scale_part = jnp.zeros((1, rows), F32)

    def weigh(t, scale_part):
        cols = pl.ds(t * rows, rows)

        def tile(i, carry):
            at = pl.ds(pl.multiple_of(i * rows, rows), rows)
            s = scores[at, cols]
            lse = row_top[at, :]
            by_row = jnp.exp(s - jnp.concatenate([lse, lse], axis=1))
            w = 0.5 * (by_row + jnp.exp(s - text_lse[t]))
            if t == 0:
                w = jnp.where(diagonal & (i == 0), w - 1.0, w)
            r_hi[at, cols], r_lo[at, cols] = split(w)
            return carry + jnp.sum(w * s, axis=0, keepdims=True)

        return lax.fori_loop(0, N_IMG, tile, scale_part, unroll=True)

    def text_partial(d, e):
        t = 2 * d + e
        cols = pl.ds(t * rows, rows)

        def part(n, carry):
            wide = pl.ds(pl.multiple_of(n * 256, 256), 256)
            acc = dot(r_hi[:, cols], img_hi[:, wide], tn)
            acc += dot(r_hi[:, cols], img_lo[:, wide], tn)
            acc += dot(r_lo[:, cols], img_hi[:, wide], tn)
            txt_part[t, :, wide] = acc
            return carry

        lax.fori_loop(0, img_ref.shape[1] // 256, part, 0)

    def image_partial(i):
        at = pl.ds(i * rows, rows)

        def part(n, carry):
            wide = pl.ds(pl.multiple_of(n * 256, 256), 256)
            acc = dot(r_hi[at, :], txt_hi[:, wide], nn)
            acc += dot(r_hi[at, :], txt_lo[:, wide], nn)
            acc += dot(r_lo[at, :], txt_hi[:, wide], nn)
            img_part[i, :, wide] = acc
            return carry

        lax.fori_loop(0, img_ref.shape[1] // 256, part, 0)

    def add(dst, src):
        dst[...] += src[...]

    def gp(d, e):
        return txt_part.at[2 * d + e]

    for t in (7, 6, 5, 4, 3, 2, 1, 0):
        scale_part = weigh(t, scale_part)

    def up(d, e, distance):
        if e == 0:
            pieces(f"a{e}", gp(d, e), ring_got.at[e], me.move(blk=distance), is1)
        else:
            pieces(f"a{e}", gp(d, e), ring_got.at[e], me.move(blk=distance), is1 & (me.z != 3))
            pieces(f"a{e}", gp(d, e), ring_got.at[e], me.move(blk=distance, h=1), is1 & at3)

    def chip(d, e):
        send(f"g{d}{e}", gp(d + 1, e), chip_got.at[2 * d + e], me.move(c=1), is0)

    def chip_add(d, e):
        arrive(f"g{d}{e}", chip_got.at[2 * d + e], is1)

        @pl.when(is1)
        def _():
            add(gp(d, e), chip_got.at[2 * d + e])

    def forward(e):
        for p, at in (("a", top), ("b", bottom)):
            arrive(f"b{e}{p}", relay_got.at[e, at], is1)
            if e == 0:
                send(f"back{e}{p}", relay_got.at[e, at], relay_back.at[e, at], back_to, is1)
            else:
                send(f"back{e}{p}", relay_got.at[e, at], relay_back.at[e, at], back_to, is1 & ~crossing)
                send(f"back{e}{p}", relay_got.at[e, at], relay_back.at[e, at], back_to.move(h=1), is1 & crossing)

    text_partial(3, 1)
    chip(2, 1)
    pieces("b1", gp(3, 1), relay_got.at[1], me.move(z=-1), is1)
    text_partial(2, 1)
    chip(1, 1)
    chip_add(2, 1)
    up(2, 1, 2)
    text_partial(1, 1)
    chip(0, 1)
    chip_add(1, 1)
    up(1, 1, 1)
    image_partial(3)
    send("p3a", img_part.at[3, top], img_half.at[0], me.move(x=1))
    send("p3b", img_part.at[3, bottom], img_half.at[1], me.move(x=-1))
    text_partial(3, 0)
    chip(2, 0)
    pieces("b0", gp(3, 0), relay_got.at[0], me.move(z=-1), is1)
    forward(1)
    image_partial(1)
    send("p1b", img_part.at[1, bottom], img_got.at[0, bottom], me.move(x=1))
    image_partial(2)
    send("p2a", img_part.at[2, top], img_got.at[1, top], me.move(x=-1))
    text_partial(2, 0)
    chip(1, 0)
    chip_add(2, 0)
    up(2, 0, 2)
    arrive("p3a", img_half.at[0])
    add(img_part.at[1, top], img_half.at[0])
    send("p1a", img_part.at[1, top], img_got.at[0, top], me.move(x=1))
    arrive("p3b", img_half.at[1])
    add(img_part.at[2, bottom], img_half.at[1])
    send("p2b", img_part.at[2, bottom], img_got.at[1, bottom], me.move(x=-1))
    text_partial(1, 0)
    chip(0, 0)
    chip_add(1, 0)
    up(1, 0, 1)
    text_partial(0, 1)
    chip_add(0, 1)
    forward(0)
    for p, at in (("a", top), ("b", bottom)):
        arrive("a1" + p, ring_got.at[1, at])

        @pl.when(not0)
        def _(at=at):
            add(gp(0, 1).at[at], ring_got.at[1, at])

        arrive("back1" + p, relay_back.at[1, at], is0)

        @pl.when(is0 & (me.z >= 2))
        def _(at=at):
            add(gp(0, 1).at[at], relay_back.at[1, at])

        send("y" + p, gp(0, 1).at[at], pair_got.at[at], me.move(h=1))
    text_partial(0, 0)
    chip_add(0, 0)

    @pl.when(at0)
    def _():
        add(gp(0, 0), ring_got.at[1])

    @pl.when(is0 & (me.z < 2))
    def _():
        add(gp(0, 0), relay_back.at[1])

    image_partial(0)

    loss_sum = jnp.sum(loss_part, axis=1, keepdims=True)
    scale_sum = jnp.sum(scale_part, axis=1, keepdims=True) / scale
    line = lax.broadcasted_iota(jnp.int32, (8, 128), 0)
    total = jnp.where(line == 0, loss_sum, scale_sum)
    stages = [
        [me.move(c=1)],
        [me.move(h=1)],
        [me.move(yl=1)],
        [me.move(x=1), me.move(x=2), me.move(x=3)],
        [me.move(z=1), me.move(z=2), me.move(z=3)],
    ]
    n = 0
    for level, peers in enumerate(stages):
        sum_send[level] = total
        for j, p in enumerate(peers):
            send(f"s{n + j}", sum_send.at[level], sum_got.at[n + j], p)
        for j in range(len(peers)):
            arrive(f"s{n + j}", sum_got.at[n + j])
            total = total + sum_got[n + j]
        n += len(peers)
    pairs = rows * lax.axis_size("blk") * lax.axis_size("row")
    sums_ref[...] = total / pairs

    arrive_pieces("a0", ring_got.at[0])
    arrive_pieces("back0", relay_back.at[0], is0)

    @pl.when(is0)
    def _():
        add(gp(0, 0), relay_back.at[0])

    for name, at, j in (("p1b", bottom, 0), ("p2a", top, 1), ("p1a", top, 0), ("p2b", bottom, 1)):
        arrive(name, img_got.at[j, at])
    img_out[...] = scale * (img_part[0] + img_got[0] + img_got[1])
    arrive_pieces("y", pair_got)
    txt_out[...] = scale * (txt_part[0] + ring_got[0] + pair_got[...])

    for c, when in [entry for entry in pending if entry is not None]:
        if when is None:
            c.wait_send()
        else:
            pl.when(when)(c.wait_send)


N_SEM = 128


def shards(image_embed, text_embed, logit_scale):
    rows, width = image_embed.shape
    block = (rows, width)
    vmem = pl.BlockSpec(memory_space=pltpu.VMEM)
    sums, image_grad, text_grad = pl.pallas_call(
        functools.partial(kernel, rows),
        out_shape=(
            jax.ShapeDtypeStruct((8, 128), F32),
            jax.ShapeDtypeStruct(block, F32),
            jax.ShapeDtypeStruct(block, F32),
        ),
        in_specs=[pl.BlockSpec(memory_space=pltpu.SMEM), vmem, vmem],
        out_specs=(vmem, vmem, vmem),
        scratch_shapes=[
            pltpu.VMEM((3, *block), F32),
            pltpu.VMEM((7, *block), F32),
            pltpu.VMEM((2, *block), F32),
            pltpu.VMEM((N_IMG * rows, width), BF16),
            pltpu.VMEM((N_IMG * rows, width), BF16),
            pltpu.VMEM((N_TXT * rows, width), BF16),
            pltpu.VMEM((N_TXT * rows, width), BF16),
            pltpu.VMEM((N_IMG * rows, N_TXT * rows), F32),
            pltpu.VMEM((N_IMG * rows, N_TXT * rows), BF16),
            pltpu.VMEM((N_IMG * rows, N_TXT * rows), BF16),
            pltpu.VMEM((N_IMG * rows, 128), F32),
            pltpu.VMEM((N_IMG * rows, 128), F32),
            pltpu.VMEM((2 * N_IMG, rows), F32),
            pltpu.VMEM((2 * N_TXT, rows), F32),
            pltpu.VMEM((3, 2 * N_IMG, rows), F32),
            pltpu.VMEM((len(DELTAS), 2 * N_TXT, rows), F32),
            pltpu.VMEM((N_IMG, *block), F32),
            pltpu.VMEM((N_TXT, *block), F32),
            pltpu.VMEM((6, *block), F32),
            pltpu.VMEM((2, *block), F32),
            pltpu.VMEM((2, *block), F32),
            pltpu.VMEM((2, *block), F32),
            pltpu.VMEM(block, F32),
            pltpu.VMEM((2, *block), F32),
            pltpu.VMEM((2, rows // 2, width), F32),
            pltpu.VMEM((5, 8, 128), F32),
            pltpu.VMEM((9, 8, 128), F32),
            pltpu.SemaphoreType.DMA((N_SEM,)),
            pltpu.SemaphoreType.DMA((N_SEM,)),
        ],
        compiler_params=pltpu.CompilerParams(
            collective_id=0, has_side_effects=True, vmem_limit_bytes=62 << 20
        ),
        cost_estimate=pl.CostEstimate(flops=29 * 10**9, bytes_accessed=4 * 10**6, transcendentals=10**7),
    )(logit_scale, image_embed, text_embed)
    return sums[0, :1], sums[1, :1], image_grad, text_grad


def solution(mesh):
    in_specs = (P(("blk", "row"), None), P(("blk", "row"), None), P())
    out_specs = (P(), P(), P(("blk", "row"), None), P(("blk", "row"), None))
    return jax.shard_map(shards, mesh=mesh, in_specs=in_specs, out_specs=out_specs, check_vma=False)
```

```python
import functools

import jax
import jax.numpy as jnp
from jax import lax
from jax.experimental import pallas as pl
from jax.experimental.pallas import tpu as pltpu
from jax.sharding import PartitionSpec as P

MESH = pl.DeviceIdType.MESH
F32 = jnp.float32
BF16 = jnp.bfloat16
WINDOW = 4
N_IMG = 4
OFFSETS = (0, 1, 3, 2)
N_TXT = 8
LOW = -1e30

DELTAS = [(d, g) for d in (-3, -2, -1, 0, 1, 2, 3) for g in (0, 1) if (d, g) != (0, 0)]


class Place:
    def __init__(self, y_lo, z, core, y_hi, x):
        self.y_lo, self.z, self.core, self.y_hi, self.x = y_lo, z, core, y_hi, x

    def device(self):
        return (self.y_lo * 8 + self.z * 2 + self.core, self.y_hi * 4 + self.x)

    def move(self, x=0, h=0, c=0, z=0, yl=0, blk=0, plane=0):
        y_lo, zz, core = self.y_lo, self.z, self.core
        if blk:
            b = lax.rem(y_lo * 8 + zz * 2 + core + blk + 16, 16)
            y_lo, zz, core = b // 8, lax.rem(b // 2, 4), lax.rem(b, 2)
        if plane:
            k = lax.rem(y_lo * 4 + zz + plane + 8, 8)
            y_lo, zz = k // 4, lax.rem(k, 4)
        if z:
            zz = lax.rem(zz + z + 4, 4)
        if c:
            core = 1 - core
        if yl:
            y_lo = 1 - y_lo
        y_hi = 1 - self.y_hi if h else self.y_hi
        xx = lax.rem(self.x + x + 4, 4) if x else self.x
        return Place(y_lo, zz, core, y_hi, xx)


def here():
    b, r = lax.axis_index("blk"), lax.axis_index("row")
    return Place(b // 8, lax.rem(b // 2, 4), lax.rem(b, 2), r // 4, lax.rem(r, 4))


def split(value):
    high = value.astype(BF16)
    return high, (value - high.astype(F32)).astype(BF16)


def kernel(
    rows,
    scale_ref,
    img_ref,
    txt_ref,
    sums_ref,
    img_out,
    txt_out,
    img_in,
    txt_in,
    relay_in,
    img_hi,
    img_lo,
    txt_hi,
    txt_lo,
    scores,
    r_hi,
    r_lo,
    row_top,
    row_sum,
    row_stat,
    col_stat,
    row_got,
    col_got,
    txt_part,
    chip_got,
    ring_got,
    relay_got,
    relay_back,
    pair_got,
    img_got,
    img_half,
    sum_send,
    sum_got,
    send_sem,
    recv_sem,
):
    me = here()
    is0, is1 = me.core == 0, me.core == 1
    half = rows // 2
    top, bottom = pl.ds(0, half), pl.ds(half, half)
    scale = scale_ref[0]
    pending = []
    slots = {}

    def sem(name):
        return slots.setdefault(name, len(slots))

    def copy(name, src, dst, place):
        return pltpu.make_async_remote_copy(
            src_ref=src,
            dst_ref=dst,
            send_sem=send_sem.at[len(pending)],
            recv_sem=recv_sem.at[sem(name)],
            device_id=place.device(),
            device_id_type=MESH,
        )

    def send(name, src, dst, place, when=None):
        c = copy(name, src, dst, place)
        if when is None:
            c.start()
        else:
            pl.when(when)(c.start)
        pending.append((c, when))

    def arrive(name, dst, when=None):
        c = copy(name, dst, dst, me.move(h=1))
        if when is None:
            c.wait_recv()
        else:
            pl.when(when)(c.wait_recv)

    def pieces(name, src, dst, place, when=None):
        send(name + "a", src.at[top], dst.at[top], place, when)
        send(name + "b", src.at[bottom], dst.at[bottom], place, when)

    def arrive_pieces(name, dst, when=None):
        arrive(name + "a", dst.at[top], when)
        arrive(name + "b", dst.at[bottom], when)

    relay_to = me.move(z=-1).move(plane=-2).move(c=1)
    relay_from = me.move(plane=2).move(z=1).move(c=1)
    back_to = me.move(z=1).move(plane=2).move(c=1)
    back_from = me.move(plane=-2).move(z=-1).move(c=1)
    crossing = (me.z == 1) | (me.z == 2)

    partners = [me.move(x=1), me.move(x=2), me.move(x=3), me.move(h=1), me.move(c=1)]
    partners += [me.move(z=1), me.move(z=2), me.move(z=3), me.move(yl=1)]
    partners += [me.move(z=-1, c=1), relay_from, relay_from.move(h=1), back_from, back_from.move(h=1)]
    partners += [me.move(blk=d, h=g) for d, g in DELTAS if d != 0]
    barrier = pltpu.get_barrier_semaphore()
    for p in partners:
        pl.semaphore_signal(barrier, inc=1, device_id=p.device(), device_id_type=MESH)
    pl.semaphore_wait(barrier, len(partners))

    def tx(d, e):
        return txt_in.at[2 * d + e - 1]

    at0 = me.z == 0
    not0 = me.z != 0
    prev = [me.move(blk=-1), me.move(blk=-2)]
    at3 = me.z == 3
    pieces("t10", txt_ref, tx(1, 0), me.move(blk=-1), is1 | not0)
    early = len(pending)
    pieces("t10", txt_ref, tx(1, 0), me.move(blk=-1), is0 & at0)
    pieces("t20", txt_ref, tx(2, 0), me.move(blk=-2), is1 & at0)
    pieces("t20", txt_ref, tx(2, 0), me.move(blk=-2), is1 & not0)
    pieces("r0", txt_ref, relay_in.at[0], me.move(z=1), is0)
    pieces("t01", txt_ref, tx(0, 1), me.move(h=1), not0)
    pieces("i1", img_ref, img_in.at[0], me.move(x=-1))
    pieces("i2", img_ref, img_in.at[1], me.move(x=1))

    def img_ready(i, value):
        high, low = split(value)
        at = pl.ds(i * rows, rows)
        img_hi[at, :] = high
        img_lo[at, :] = low

    def txt_ready(t, value):
        high, low = split(value)
        at = pl.ds(t * rows, rows)
        txt_hi[at, :] = high
        txt_lo[at, :] = low

    row_top[...] = jnp.full(row_top.shape, LOW, F32)
    row_sum[...] = jnp.zeros(row_sum.shape, F32)
    img_ready(0, img_ref[...])
    txt_ready(0, txt_ref[...])

    nt = (((1,), (1,)), ((), ()))
    tn = (((0,), (0,)), ((), ()))
    nn = (((1,), (0,)), ((), ()))

    def dot(a, b, dims):
        return lax.dot_general(a, b, dims, preferred_element_type=F32)

    def score_tiles(t, first, last):
        cols = pl.ds(t * rows, rows)

        def tile(i, carry):
            at = pl.ds(pl.multiple_of(i * rows, rows), rows)
            raw = dot(img_hi[at, :], txt_hi[cols, :], nt)
            raw += dot(img_hi[at, :], txt_lo[cols, :], nt)
            raw += dot(img_lo[at, :], txt_hi[cols, :], nt)
            scores[at, cols] = scale * raw
            return carry

        lax.fori_loop(first, last, tile, 0, unroll=True)

    def block_stats(t):
        cols = pl.ds(t * rows, rows)

        def tops(i, carry):
            at = pl.ds(pl.multiple_of(i * rows, rows), rows)
            s = scores[at, cols]
            s0, s1 = s[:, :128], s[:, 128:]
            old = row_top[at, :]
            new = jnp.maximum(old, jnp.maximum(s0, s1))
            row_sum[at, :] = (
                row_sum[at, :] * jnp.exp(old - new) + jnp.exp(s0 - new) + jnp.exp(s1 - new)
            )
            row_top[at, :] = new
            return jnp.maximum(carry, jnp.max(s, axis=0, keepdims=True))

        ctop = lax.fori_loop(0, N_IMG, tops, jnp.full((1, rows), LOW, F32), unroll=True)

        def totals(i, carry):
            at = pl.ds(pl.multiple_of(i * rows, rows), rows)
            return carry + jnp.sum(jnp.exp(scores[at, cols] - ctop), axis=0, keepdims=True)

        csum = lax.fori_loop(0, N_IMG, totals, jnp.zeros((1, rows), F32), unroll=True)
        col_stat[t : t + 1, :] = ctop
        col_stat[N_TXT + t : N_TXT + t + 1, :] = csum

    def text_block(d, e):
        arrive_pieces(f"t{d}{e}", tx(d, e))
        txt_ready(2 * d + e, tx(d, e)[...])

    def scored(t):
        score_tiles(t, 0, N_IMG)
        block_stats(t)

    score_tiles(0, 0, 1)
    for p, at in (("a", top), ("b", bottom)):
        arrive("r0" + p, relay_in.at[0, at], is0)
        send("t30" + p, relay_in.at[0, at], tx(3, 0).at[at], relay_to, is0)
        send("t31" + p, relay_in.at[0, at], tx(3, 1).at[at], relay_to.move(h=1), is0 & crossing)
    for i in range(early, early + 4):
        c, when = pending[i]
        pl.when(when)(c.wait_send)
        pending[i] = None
    pieces("t01", txt_ref, tx(0, 1), me.move(h=1), at0)
    for p, at in (("a", top), ("b", bottom)):
        arrive("t01" + p, tx(0, 1).at[at])
        send("t11" + p, tx(0, 1).at[at], tx(1, 1).at[at], me.move(blk=-1), is1 | not0)
        send("t21" + p, tx(0, 1).at[at], tx(2, 1).at[at], me.move(blk=-2), is1 & not0)
        send("r1" + p, tx(0, 1).at[at], relay_in.at[1, at], me.move(z=1), is0 & (me.z >= 2))
    arrive("i1a", img_in.at[0, top])
    send("i3a", img_in.at[0, top], img_in.at[2, top], me.move(x=-1))
    arrive("i2b", img_in.at[1, bottom])
    send("i3b", img_in.at[1, bottom], img_in.at[2, bottom], me.move(x=1))
    txt_ready(1, tx(0, 1)[...])
    score_tiles(1, 0, 1)
    for d in (1, 2):
        for p, at in (("a", top), ("b", bottom)):
            arrive(f"t{d}0{p}", tx(d, 0).at[at])
            send(f"t{d + 1}0{p}", tx(d, 0).at[at], tx(d + 1, 0).at[at], me.move(c=1), is1)
            send(f"t{d}1{p}", tx(d, 0).at[at], tx(d, 1).at[at], me.move(h=1), is1 & at3)
        txt_ready(2 * d, tx(d, 0)[...])
    arrive("i1b", img_in.at[0, bottom])
    arrive("i2a", img_in.at[1, top])
    img_ready(1, img_in[0])
    img_ready(2, img_in[1])
    score_tiles(0, 1, 3)
    score_tiles(1, 1, 3)
    for p, at in (("a", top), ("b", bottom)):
        arrive("r1" + p, relay_in.at[1, at], is0 & ~crossing)
        send("t31" + p, relay_in.at[1, at], tx(3, 1).at[at], relay_to, is0 & ~crossing)
    arrive("i3a", img_in.at[2, top])
    arrive("i3b", img_in.at[2, bottom])
    img_ready(3, img_in[2])
    for t in (0, 1):
        score_tiles(t, 3, 4)
        block_stats(t)
    scored(2)
    scored(4)
    text_block(3, 0)
    scored(6)
    text_block(1, 1)
    pieces("t21", tx(1, 1), tx(2, 1), me.move(c=1), is1)
    text_block(2, 1)
    pieces("t31", tx(2, 1), tx(3, 1), me.move(c=1), is1)
    scored(3)
    scored(5)
    text_block(3, 1)
    scored(7)

    for n, (d, g) in enumerate(DELTAS):
        m = DELTAS.index((-d, g))
        send(f"c{m}", col_stat, col_got.at[m], me.move(blk=d, h=g))
    for i in range(N_IMG):
        at = pl.ds(i * rows, rows)
        m = jnp.transpose(row_top[at, :])
        s = jnp.transpose(row_sum[at, :])
        best = jnp.max(m, axis=0, keepdims=True)
        row_stat[i : i + 1, :] = best
        row_stat[N_IMG + i : N_IMG + i + 1, :] = jnp.sum(s * jnp.exp(m - best), axis=0, keepdims=True)
    for o in (1, 2, 3):
        send(f"r{4 - o}", row_stat, row_got.at[4 - o - 1], me.move(x=o))
    for n in range(len(DELTAS)):
        arrive(f"c{n}", col_got.at[n])
    for o in (1, 2, 3):
        arrive(f"r{o}", row_got.at[o - 1])

    def join(parts):
        best = functools.reduce(jnp.maximum, [m for m, _ in parts])
        return best + jnp.log(sum(s * jnp.exp(m - best) for m, s in parts))

    text_lse = []
    for t in range(N_TXT):
        d, e = t // 2, t % 2
        parts = [(col_stat[t : t + 1, :], col_stat[N_TXT + t : N_TXT + t + 1, :])]
        for n, (dd, g) in enumerate(DELTAS):
            if 0 <= d - dd < WINDOW:
                u = 2 * (d - dd) + (1 - e if g else e)
                parts.append((col_got[n, u : u + 1, :], col_got[n, N_TXT + u : N_TXT + u + 1, :]))
        text_lse.append(join(parts))
    loss_part = 0.5 * text_lse[0]
    for i in range(N_IMG):
        parts = [(row_stat[i : i + 1, :], row_stat[N_IMG + i : N_IMG + i + 1, :])]
        for o in (1, 2, 3):
            u = OFFSETS.index((OFFSETS[i] - o) % 4)
            parts.append((row_got[o - 1, u : u + 1, :], row_got[o - 1, N_IMG + u : N_IMG + u + 1, :]))
        lse = join(parts)
        if i == 0:
            loss_part += 0.5 * lse
        row_top[pl.ds(i * rows, rows), :] = jnp.transpose(jnp.broadcast_to(lse, (128, rows)))

    diagonal = lax.broadcasted_iota(jnp.int32, (rows, rows), 0) == lax.broadcasted_iota(
        jnp.int32, (rows, rows), 1
    )
    own = scores[pl.ds(0, rows), pl.ds(0, rows)]
    loss_part -= jnp.sum(jnp.where(diagonal, own, 0.0), axis=0, keepdims=True)
    scale_part = jnp.zeros((1, rows), F32)

    def weigh(t, scale_part):
        cols = pl.ds(t * rows, rows)

        def tile(i, carry):
            at = pl.ds(pl.multiple_of(i * rows, rows), rows)
            s = scores[at, cols]
            lse = row_top[at, :]
            by_row = jnp.exp(s - jnp.concatenate([lse, lse], axis=1))
            w = 0.5 * (by_row + jnp.exp(s - text_lse[t]))
            if t == 0:
                w = jnp.where(diagonal & (i == 0), w - 1.0, w)
            r_hi[at, cols], r_lo[at, cols] = split(w)
            return carry + jnp.sum(w * s, axis=0, keepdims=True)

        return lax.fori_loop(0, N_IMG, tile, scale_part, unroll=True)

    def text_partial(d, e):
        t = 2 * d + e
        cols = pl.ds(t * rows, rows)

        acc = dot(r_hi[:, cols], img_hi[...], tn)
        acc += dot(r_hi[:, cols], img_lo[...], tn)
        acc += dot(r_lo[:, cols], img_hi[...], tn)
        txt_part[t] = acc

    def image_partial(i):
        at = pl.ds(i * rows, rows)

        def part(n, carry):
            wide = pl.ds(pl.multiple_of(n * 256, 256), 256)
            acc = dot(r_hi[at, :], txt_hi[:, wide], nn)
            acc += dot(r_hi[at, :], txt_lo[:, wide], nn)
            acc += dot(r_lo[at, :], txt_hi[:, wide], nn)
            scores[at, wide] = acc
            return carry

        lax.fori_loop(0, img_ref.shape[1] // 256, part, 0)

    def add(dst, src):
        dst[...] += src[...]

    def held(i, at):
        return scores.at[pl.ds(i * rows + at.start, at.size), pl.ds(0, img_ref.shape[1])]

    def gp(d, e):
        return txt_part.at[2 * d + e]

    for t in (7, 6, 5, 4, 3, 2, 1, 0):
        scale_part = weigh(t, scale_part)

    def up(d, e, distance):
        pieces(f"a{e}", gp(d, e), ring_got.at[e], me.move(blk=distance), is1 & (me.z != 3))
        if e == 1:
            pieces(f"q{d}", gp(d, 1), relay_back.at[d - 1], me.move(h=1), is1 & at3)
        else:
            for p, at in (("a", top), ("b", bottom)):
                arrive(f"q{d}{p}", relay_back.at[d - 1, at], is1 & at3)

                @pl.when(is1 & at3)
                def _(at=at):
                    add(gp(d, 0).at[at], relay_back.at[d - 1, at])

                place = me.move(z=1) if d == 2 else me.move(z=1, c=1)
                send("a1" + p, gp(d, 0).at[at], ring_got.at[1, at], place, is1 & at3)

    def cross(p, at):
        arrive("a1" + p, ring_got.at[1, at], at0)
        send("a0" + p, ring_got.at[1, at], ring_got.at[0, at], me.move(yl=1), at0)

    def chip(d, e):
        send(f"g{d}{e}", gp(d + 1, e), chip_got.at[2 * d + e], me.move(c=1), is0)

    def chip_add(d, e):
        arrive(f"g{d}{e}", chip_got.at[2 * d + e], is1)

        @pl.when(is1)
        def _():
            add(gp(d, e), chip_got.at[2 * d + e])

    def forward(e):
        for p, at in (("a", top), ("b", bottom)):
            arrive(f"b{e}{p}", relay_got.at[e, at], is1)
            if e == 0:
                send(f"back{e}{p}", relay_got.at[e, at], relay_back.at[e, at], back_to, is1)
            else:
                send(f"back{e}{p}", relay_got.at[e, at], relay_back.at[e, at], back_to, is1 & ~crossing)
                send(f"back{e}{p}", relay_got.at[e, at], relay_back.at[e, at], back_to.move(h=1), is1 & crossing)

    text_partial(3, 1)
    chip(2, 1)
    pieces("b1", gp(3, 1), relay_got.at[1], me.move(z=-1), is1)
    text_partial(2, 1)
    chip(1, 1)
    chip_add(2, 1)
    up(2, 1, 2)
    text_partial(1, 1)
    chip(0, 1)
    chip_add(1, 1)
    up(1, 1, 1)
    text_partial(0, 1)
    chip_add(0, 1)
    pieces("y", gp(0, 1), pair_got, me.move(h=1), at0)
    image_partial(3)
    send("p3a", held(3, top), img_half.at[0], me.move(x=1))
    send("p3b", held(3, bottom), img_half.at[1], me.move(x=-1))
    text_partial(3, 0)
    chip(2, 0)
    pieces("b0", gp(3, 0), relay_got.at[0], me.move(z=-1), is1)
    forward(1)
    image_partial(1)
    send("p1b", held(1, bottom), img_got.at[0, bottom], me.move(x=1))
    image_partial(2)
    send("p2a", held(2, top), img_got.at[1, top], me.move(x=-1))
    text_partial(2, 0)
    chip(1, 0)
    chip_add(2, 0)
    up(2, 0, 2)
    arrive("p3a", img_half.at[0])
    add(held(1, top), img_half.at[0])
    send("p1a", held(1, top), img_got.at[0, top], me.move(x=1))
    arrive("p3b", img_half.at[1])
    add(held(2, bottom), img_half.at[1])
    send("p2b", held(2, bottom), img_got.at[1, bottom], me.move(x=-1))
    text_partial(1, 0)
    chip(0, 0)
    chip_add(1, 0)
    up(1, 0, 1)
    forward(0)
    for p, at in (("a", top), ("b", bottom)):
        arrive("a1" + p, ring_got.at[1, at], not0)

        @pl.when(not0)
        def _(at=at):
            add(gp(0, 1).at[at], ring_got.at[1, at])

        arrive("back1" + p, relay_back.at[1, at], is0)

        @pl.when(is0 & (me.z >= 2))
        def _(at=at):
            add(gp(0, 1).at[at], relay_back.at[1, at])

        send("y" + p, gp(0, 1).at[at], pair_got.at[at], me.move(h=1), not0)
    cross("a", top)
    text_partial(0, 0)
    chip_add(0, 0)
    cross("b", bottom)

    @pl.when(is0 & (me.z < 2))
    def _():
        add(gp(0, 0), relay_back.at[1])

    image_partial(0)

    loss_sum = jnp.sum(loss_part, axis=1, keepdims=True)
    scale_sum = jnp.sum(scale_part, axis=1, keepdims=True) / scale
    line = lax.broadcasted_iota(jnp.int32, (8, 128), 0)
    total = jnp.where(line == 0, loss_sum, scale_sum)
    stages = [
        [me.move(c=1)],
        [me.move(h=1)],
        [me.move(yl=1)],
        [me.move(x=1), me.move(x=2), me.move(x=3)],
        [me.move(z=1), me.move(z=2), me.move(z=3)],
    ]
    n = 0
    for level, peers in enumerate(stages):
        sum_send[level] = total
        for j, p in enumerate(peers):
            send(f"s{n + j}", sum_send.at[level], sum_got.at[n + j], p)
        for j in range(len(peers)):
            arrive(f"s{n + j}", sum_got.at[n + j])
            total = total + sum_got[n + j]
        n += len(peers)
    pairs = rows * lax.axis_size("blk") * lax.axis_size("row")
    sums_ref[...] = total / pairs

    arrive_pieces("a0", ring_got.at[0])
    arrive_pieces("back0", relay_back.at[0], is0)

    @pl.when(is0)
    def _():
        add(gp(0, 0), relay_back.at[0])

    for name, at, j in (("p1b", bottom, 0), ("p2a", top, 1), ("p1a", top, 0), ("p2b", bottom, 1)):
        arrive(name, img_got.at[j, at])
    img_out[...] = scale * (held(0, pl.ds(0, rows))[...] + img_got[0] + img_got[1])
    arrive_pieces("y", pair_got)
    txt_out[...] = scale * (txt_part[0] + ring_got[0] + pair_got[...])

    for c, when in [entry for entry in pending if entry is not None]:
        if when is None:
            c.wait_send()
        else:
            pl.when(when)(c.wait_send)


N_SEM = 128


def shards(image_embed, text_embed, logit_scale):
    rows, width = image_embed.shape
    block = (rows, width)
    vmem = pl.BlockSpec(memory_space=pltpu.VMEM)
    sums, image_grad, text_grad = pl.pallas_call(
        functools.partial(kernel, rows),
        out_shape=(
            jax.ShapeDtypeStruct((8, 128), F32),
            jax.ShapeDtypeStruct(block, F32),
            jax.ShapeDtypeStruct(block, F32),
        ),
        in_specs=[pl.BlockSpec(memory_space=pltpu.SMEM), vmem, vmem],
        out_specs=(vmem, vmem, vmem),
        scratch_shapes=[
            pltpu.VMEM((3, *block), F32),
            pltpu.VMEM((7, *block), F32),
            pltpu.VMEM((2, *block), F32),
            pltpu.VMEM((N_IMG * rows, width), BF16),
            pltpu.VMEM((N_IMG * rows, width), BF16),
            pltpu.VMEM((N_TXT * rows, width), BF16),
            pltpu.VMEM((N_TXT * rows, width), BF16),
            pltpu.VMEM((N_IMG * rows, N_TXT * rows), F32),
            pltpu.VMEM((N_IMG * rows, N_TXT * rows), BF16),
            pltpu.VMEM((N_IMG * rows, N_TXT * rows), BF16),
            pltpu.VMEM((N_IMG * rows, 128), F32),
            pltpu.VMEM((N_IMG * rows, 128), F32),
            pltpu.VMEM((2 * N_IMG, rows), F32),
            pltpu.VMEM((2 * N_TXT, rows), F32),
            pltpu.VMEM((3, 2 * N_IMG, rows), F32),
            pltpu.VMEM((len(DELTAS), 2 * N_TXT, rows), F32),
            pltpu.VMEM((N_TXT, *block), F32),
            pltpu.VMEM((6, *block), F32),
            pltpu.VMEM((2, *block), F32),
            pltpu.VMEM((2, *block), F32),
            pltpu.VMEM((2, *block), F32),
            pltpu.VMEM(block, F32),
            pltpu.VMEM((2, *block), F32),
            pltpu.VMEM((2, rows // 2, width), F32),
            pltpu.VMEM((5, 8, 128), F32),
            pltpu.VMEM((9, 8, 128), F32),
            pltpu.SemaphoreType.DMA((N_SEM,)),
            pltpu.SemaphoreType.DMA((N_SEM,)),
        ],
        compiler_params=pltpu.CompilerParams(
            collective_id=0, has_side_effects=True, vmem_limit_bytes=62 << 20
        ),
        cost_estimate=pl.CostEstimate(flops=29 * 10**9, bytes_accessed=4 * 10**6, transcendentals=10**7),
    )(logit_scale, image_embed, text_embed)
    return sums[0, :1], sums[1, :1], image_grad, text_grad


def solution(mesh):
    in_specs = (P(("blk", "row"), None), P(("blk", "row"), None), P())
    out_specs = (P(), P(), P(("blk", "row"), None), P(("blk", "row"), None))
    return jax.shard_map(shards, mesh=mesh, in_specs=in_specs, out_specs=out_specs, check_vma=False)
```
